32 devices in a mesh: dp: 8 (over z, y), tensor: 4 (over x, core).
Axes of the slice: x: 2, y: 2, z: 4, core: 2. Of those that a mesh axis runs over, the one named last changes fastest.
Arguments:
- layer_input: bfloat16 [4096, 1024], P(('dp', 'tensor')), may hold values from -6 to 6
- segments: int32 [4096], P('dp'), may hold values from 0 to 23, as said below
- positions: int32 [4096], P('dp'), may hold values from 0 to 1535, as said below
- first_gain: float32 [1024], replicated, may hold values from 0.5 to 1.5
- merged_weight: bfloat16 [1024, 3, 1024], P('dp', None, 'tensor'), may hold values from -0.1875 to 0.1875
- output_weight: bfloat16 [1024, 1024], P('tensor', 'dp'), may hold values from -1 to 1
- second_gain: float32 [1024], replicated, may hold values from 0.5 to 1.5
- expand_weight: bfloat16 [1024, 2, 2624], P('dp', None, 'tensor'), may hold values from -0.1875 to 0.1875
- shrink_weight: bfloat16 [2624, 1024], P('tensor', 'dp'), may hold values from -0.125 to 0.125
- cotangent: bfloat16 [4096, 1024], P(('dp', 'tensor')), may hold values from -6 to 6
Outputs:
- layer_output: bfloat16 [4096, 1024], P(('dp', 'tensor'))
- input_grad: float32 [4096, 1024], P(('dp', 'tensor'))
- first_gain_grad: float32 [1024], replicated
- merged_grad: float32 [1024, 3, 1024], P('dp', None, 'tensor')
- output_grad: float32 [1024, 1024], P('tensor', 'dp')
- second_gain_grad: float32 [1024], replicated
- expand_grad: float32 [1024, 2, 2624], P('dp', None, 'tensor')
- shrink_grad: float32 [2624, 1024], P('tensor', 'dp')
The draws below stay inside these ranges and needn't reach their ends.
Inputs may be any that keep to these rules, and one draw needn't show every extreme that they name: `segments`: numbers never fall along the tokens; the block of 512 tokens with index g holds the numbers 3 g, 3 g + 1 and 3 g + 2, each on one token or more. Within a document the positions rise by one from token to token.
All inputs are finite; a program needn't handle non-finite values.
Results may differ from the reference program's by a relative error of at most 0.018.
Values may be sent and summed in bfloat16 or wider, within the bound.
A program may use at most 128 MiB of HBM per device.

```python
import jax
import jax.numpy as jnp
from jax import lax

D = 1024
HEADS = 16
FF = 2624
WINDOW = 128
TOK_DEV = 128
HEAD_DIM = 64
TOK_GRP = 512
QBLK = 512
TOKENS = 4096


def cut_points(key):
    groups = TOKENS // TOK_GRP
    first_cut = jax.random.randint(jax.random.fold_in(key, 11), (groups,), 1, TOK_DEV)
    second_cut = jax.random.randint(jax.random.fold_in(key, 12), (groups,), TOK_GRP - TOK_DEV + 1, TOK_GRP)
    local = jnp.arange(TOK_GRP, dtype=jnp.int32)
    level = (local[None, :] >= first_cut[:, None]).astype(jnp.int32) + (local[None, :] >= second_cut[:, None]).astype(jnp.int32)
    return (first_cut, second_cut, level)


def draw_segments(key, part):
    first_cut, second_cut, level = cut_points(key)
    groups = TOKENS // TOK_GRP
    numbers = level + 3 * jnp.arange(groups, dtype=jnp.int32)[:, None]
    return numbers.reshape(TOKENS)


def draw_positions(key, part):
    first_cut, second_cut, level = cut_points(key)
    key = jax.random.fold_in(key, 5)
    groups = TOKENS // TOK_GRP
    offsets = jax.random.randint(key, (groups, 3), 0, 1024).astype(jnp.int32)
    offsets = offsets.at[0, 0].set(0)
    offsets = offsets.at[0, 2].set((1024 + second_cut[0]).astype(jnp.int32))
    starts = jnp.stack([jnp.zeros_like(first_cut), first_cut, second_cut], axis=1).astype(jnp.int32)
    local = jnp.arange(TOK_GRP, dtype=jnp.int32)[None, :]
    doc_offset = jnp.take_along_axis(offsets, level, axis=1)
    doc_start = jnp.take_along_axis(starts, level, axis=1)
    return (doc_offset + local - doc_start).astype(jnp.int32).reshape(TOKENS)


def block_levels(key, dims, cuts, least, high):
    loudness, own = 1.0, jax.random.fold_in(key, 6)
    for position, shards_of in cuts:
        heights = jnp.exp(jax.random.uniform(jax.random.fold_in(own, position), (shards_of,), jnp.float32, least / len(cuts), high / len(cuts)))
        loudness = loudness * jnp.repeat(heights, dims[position] // shards_of).reshape([-1 if axis == position else 1 for axis in range(len(dims))])
    return loudness


def scatter_about(stream_key, extent, width, bound, split=(), kind=jnp.bfloat16):
    entries = width * jax.random.normal(stream_key, extent, jnp.float32)
    if split:
        entries = entries * block_levels(stream_key, extent, split, -0.22, 0.18)
    return jnp.clip(entries, -bound, bound).astype(kind)


def setup_inputs(seed: int = 0) -> dict:
    keys = jax.random.split(jax.random.key(seed), 11)
    layer_input = scatter_about(keys[0], (TOKENS, D), 1.0, 6.0, ((0, 32),))
    segments = draw_segments(jax.random.fold_in(keys[10], 71), 0)
    positions = draw_positions(jax.random.fold_in(keys[10], 71), 0)
    first_gain = jnp.clip(1.0 + 0.1 * jax.random.normal(keys[3], (D,), jnp.float32), 0.5, 1.5)
    merged_weight = scatter_about(keys[4], (D, 3, D), D ** -0.5, 0.1875, ((0, 8), (2, 4)))
    output_weight = scatter_about(keys[5], (D, D), (D // 32) ** -0.5, 1.0, ((0, 4), (1, 8)))
    second_gain = jnp.clip(1.0 + 0.1 * jax.random.normal(keys[6], (D,), jnp.float32), 0.5, 1.5)
    expand_weight = scatter_about(keys[7], (D, 2, FF), D ** -0.5, 0.1875, ((0, 8), (2, 4)))
    shrink_weight = scatter_about(keys[8], (FF, D), FF ** -0.5, 0.125, ((0, 4), (1, 8)))
    cotangent = scatter_about(keys[9], (TOKENS, D), 1.0, 6.0, ((0, 32),))
    return dict(layer_input=layer_input, segments=segments, positions=positions, first_gain=first_gain, merged_weight=merged_weight, output_weight=output_weight, second_gain=second_gain, expand_weight=expand_weight, shrink_weight=shrink_weight, cotangent=cotangent)


@jax.custom_vjp
def low(v):
    return lax.optimization_barrier(v.astype(jnp.bfloat16)).astype(jnp.float32)

@jax.custom_vjp
def low_back(v):
    return v

def low_keep(v):
    return (low(v), None)

def low_pass(kept, grad):
    return (grad,)

def back_keep(v):
    return (v, None)

def back_low(kept, grad):
    return (low(grad),)
low.defvjp(low_keep, low_pass)
low_back.defvjp(back_keep, back_low)
epsilon = 1e-05
rope_base = 10000.0
precise = lax.Precision.HIGHEST
masked_score = -1e+30

def layer_norm(layer_rows, gain):
    center = layer_rows - lax.optimization_barrier(jnp.mean(layer_rows, axis=-1, keepdims=True))
    inverse = lax.rsqrt(lax.optimization_barrier(jnp.mean(center * center, axis=-1, keepdims=True)) + epsilon)
    return center * inverse * gain

def rope_tables(positions):
    half_dim = HEAD_DIM // 2
    frequency = rope_base ** (-2.0 * jnp.arange(half_dim, dtype=jnp.float32) / HEAD_DIM)
    angles = positions.astype(jnp.float32)[:, None] * frequency[None, :]
    return (jnp.cos(angles), jnp.sin(angles))

def rotate(head_rows, cosine_table, sine_table):
    half_dim = head_rows.shape[-1] // 2
    first_half = head_rows[..., :half_dim]
    second_half = head_rows[..., half_dim:]
    cosine_b = cosine_table[:, None, :]
    sine_b = sine_table[:, None, :]
    return jnp.concatenate([first_half * cosine_b - second_half * sine_b, second_half * cosine_b + first_half * sine_b], axis=-1)

def band_attention(queries, keys_rot, value_rows, segments):
    group_size = queries.shape[0]
    half_window = WINDOW // 2
    pad_spec = ((half_window, half_window), (0, 0), (0, 0))
    keys_pad = jnp.pad(keys_rot, pad_spec)
    values_pad = jnp.pad(value_rows, pad_spec)
    seg_pad = jnp.pad(segments, (half_window, half_window), constant_values=-1)
    score_scale = HEAD_DIM ** (-0.5)

    def one_block(block_index):
        offset = block_index * QBLK
        query_blk = lax.dynamic_slice_in_dim(queries, offset, QBLK, 0)
        key_blk = lax.dynamic_slice_in_dim(keys_pad, offset, QBLK + WINDOW, 0)
        value_blk = lax.dynamic_slice_in_dim(values_pad, offset, QBLK + WINDOW, 0)
        raw_scores = low_back(jnp.einsum('qhd,khd->hqk', query_blk, key_blk, precision=precise))
        rows_at = offset + jnp.arange(QBLK, dtype=jnp.int32)
        cols_at = offset - half_window + jnp.arange(QBLK + WINDOW, dtype=jnp.int32)
        seg_rows = lax.dynamic_slice_in_dim(segments, offset, QBLK, 0)
        seg_cols = lax.dynamic_slice_in_dim(seg_pad, offset, QBLK + WINDOW, 0)
        allowed = (seg_rows[:, None] == seg_cols[None, :]) & (jnp.abs(rows_at[:, None] - cols_at[None, :]) <= half_window)
        scores = jnp.where(allowed[None], raw_scores * score_scale, masked_score)
        row_max = lax.optimization_barrier(jnp.max(scores, axis=-1, keepdims=True))
        weights = jnp.exp(scores - row_max)
        softmax_out = weights / lax.optimization_barrier(jnp.sum(weights, axis=-1, keepdims=True))
        return jnp.einsum('hqk,khd->qhd', low(softmax_out), value_blk, precision=precise)
    attended = lax.map(jax.checkpoint(one_block), jnp.arange(group_size // QBLK, dtype=jnp.int32))
    return attended.reshape(group_size, HEADS, HEAD_DIM)

def group_layer(layer_rows, seg_group, pos_group, first_gain, merged_weight, output_weight, second_gain, expand_weight, shrink_weight):
    group_size = layer_rows.shape[0]
    normed = low(layer_norm(layer_rows, first_gain))
    merged_rows = low_back(jnp.einsum('td,dcf->tcf', normed, merged_weight, precision=precise))
    merged_rows = merged_rows.reshape(group_size, 3, HEADS, HEAD_DIM)
    cosine_table, sine_table = rope_tables(pos_group)
    queries = low(rotate(merged_rows[:, 0], cosine_table, sine_table))
    keys_rot = low(rotate(merged_rows[:, 1], cosine_table, sine_table))
    value_rows = low(merged_rows[:, 2])
    attended = band_attention(queries, keys_rot, value_rows, seg_group)
    attended = low_back(low(attended.reshape(group_size, D)))
    middle = layer_rows + low_back(jnp.dot(attended, output_weight, precision=precise))
    normed_two = low(layer_norm(middle, second_gain))
    gate_up = low_back(jnp.einsum('td,dcf->tcf', normed_two, expand_weight, precision=precise))
    hidden = low(jax.nn.gelu(gate_up[:, 0], approximate=False) * gate_up[:, 1])
    return middle + low_back(jnp.dot(hidden, shrink_weight, precision=precise))

def forward(layer_rows, first_gain, merged_weight, output_weight, second_gain, expand_weight, shrink_weight, segments, positions):
    groups = TOKENS // TOK_GRP

    def step(carried, inputs):
        rows_group, seg_group, pos_group = inputs
        return (carried, group_layer(rows_group, seg_group, pos_group, first_gain, merged_weight, output_weight, second_gain, expand_weight, shrink_weight))
    grouped = (layer_rows.reshape(groups, TOK_GRP, D), segments.reshape(groups, TOK_GRP), positions.reshape(groups, TOK_GRP))
    unused, result = lax.scan(jax.checkpoint(step), jnp.zeros((), jnp.float32), grouped)
    return result.reshape(TOKENS, D)

def reference(layer_input, segments, positions, first_gain, merged_weight, output_weight, second_gain, expand_weight, shrink_weight, cotangent):
    floats = (layer_input.astype(jnp.float32), first_gain.astype(jnp.float32), merged_weight.astype(jnp.float32), output_weight.astype(jnp.float32), second_gain.astype(jnp.float32), expand_weight.astype(jnp.float32), shrink_weight.astype(jnp.float32))

    def closed(layer_rows, gain_a, weight_a, weight_b, gain_b, weight_c, weight_d):
        return forward(layer_rows, gain_a, weight_a, weight_b, gain_b, weight_c, weight_d, segments, positions)
    result, pullback = jax.vjp(closed, *floats)
    grads = pullback(cotangent.astype(jnp.float32))
    return (result.astype(jnp.bfloat16), grads[0], grads[1], grads[2], grads[3], grads[4], grads[5], grads[6])
```

```python
from functools import partial

import jax
import jax.numpy as jnp
from jax import lax
from jax.experimental import pallas as pl
from jax.experimental.pallas import tpu as pltpu
from jax.sharding import PartitionSpec as P

WINDOW = 128
HEAD_DIM = 64
MESH = pl.DeviceIdType.MESH

epsilon = 1e-05
rope_base = 10000.0
masked_score = -1e30
BF = jnp.bfloat16
F32 = jnp.float32


def dot(a, b, dims=((1,), (0,))):
    return lax.dot_general(a, b, (dims, ((), ())), preferred_element_type=F32)


def normalize(rows):
    center = rows - jnp.mean(rows, axis=-1, keepdims=True)
    inverse = lax.rsqrt(jnp.mean(center * center, axis=-1, keepdims=True) + epsilon)
    return center * inverse, inverse


def norm_back(grad, hat, inverse, gain):
    gain_term = jnp.sum(grad * hat, axis=0, keepdims=True)
    grad_hat = grad * gain
    mean_grad = jnp.mean(grad_hat, axis=-1, keepdims=True)
    mean_cross = jnp.mean(grad_hat * hat, axis=-1, keepdims=True)
    return (grad_hat - mean_grad - hat * mean_cross) * inverse, gain_term


def swap_halves(rows):
    half = HEAD_DIM // 2
    width = rows.shape[1]
    lane = lax.broadcasted_iota(jnp.int32, rows.shape, 1)
    ahead = pltpu.roll(rows, width - half, 1)
    behind = pltpu.roll(rows, half, 1)
    return jnp.where(lane % HEAD_DIM < half, ahead, behind)


def key_start(block, rows, group, wide):
    return max(0, min(block * rows - WINDOW // 2, group - wide))


def band_probs(q, k, seg_q, seg_k, q_at, k_at):
    raw = dot(q, k, ((1,), (1,))) * HEAD_DIM ** (-0.5)
    row = q_at + lax.broadcasted_iota(jnp.int32, raw.shape, 0)
    col = k_at + lax.broadcasted_iota(jnp.int32, raw.shape, 1)
    ok = (seg_q == seg_k) & (jnp.abs(row - col) <= WINDOW // 2)
    score = jnp.where(ok, raw, masked_score)
    weight = jnp.exp(score - jnp.max(score, axis=-1, keepdims=True))
    return weight / jnp.sum(weight, axis=-1, keepdims=True)


class Place:
    def __init__(self, dp, tn):
        self.dp, self.tn = dp, tn
        self.d, self.t = lax.axis_index("dp"), lax.axis_index("tensor")
        self.outer = dp // 2
        self.o, self.i = self.d // 2, self.d % 2
        self.x, self.c = self.t // 2, self.t % 2
        self.core = (self.d, self.x * 2 + 1 - self.c)
        self.across = (self.d, (1 - self.x) * 2 + self.c)
        self.y = (self.o * 2 + 1 - self.i, self.t)

    def ahead(self, s):
        return (self.o + s) % self.outer

    def back(self, s):
        return (self.o + self.outer - s) % self.outer

    def z(self, s):
        return (self.ahead(s) * 2 + self.i, self.t)

    def barrier(self):
        sem = pltpu.get_barrier_semaphore()
        peers = [self.core, self.across, self.y]
        peers += [self.z(s) for s in range(1, self.outer)]
        for peer in peers:
            pl.semaphore_signal(sem, inc=1, device_id=peer, device_id_type=MESH)
        pl.semaphore_wait(sem, len(peers))


def send(src, dst, sems, index, peer):
    copy = pltpu.make_async_remote_copy(
        src_ref=src,
        dst_ref=dst,
        send_sem=sems.at[0, index],
        recv_sem=sems.at[1, index],
        device_id=peer,
        device_id_type=MESH,
    )
    copy.start()
    return copy


class TensorGather:
    def __init__(self, place, full, sems, base):
        p = self.p = place
        self.full, self.sems, self.base = full, sems, base
        self.first = send(full.at[p.t], full.at[p.t], sems, base, p.across)
        self.second = send(full.at[p.t], full.at[p.t], sems, base + 1, p.core)

    def forward(self):
        p = self.p
        self.first.wait_recv()
        at = p.across[1]
        self.third = send(self.full.at[at], self.full.at[at], self.sems, self.base + 2, p.core)

    def finish(self):
        self.second.wait_recv()
        self.third.wait_recv()
        for copy in (self.first, self.second, self.third):
            copy.wait_send()


class TensorScatter:
    def __init__(self, place, part, cbuf, held, xbuf, sems, base):
        p = self.p = place
        self.part, self.cbuf, self.held, self.xbuf = part, cbuf, held, xbuf
        self.sems, self.base = sems, base
        self.far = send(part.at[(1 - p.x) * 2 + 1 - p.c], cbuf.at[0], sems, base, p.core)
        self.near = send(part.at[p.x * 2 + 1 - p.c], cbuf.at[1], sems, base + 1, p.core)

    def forward(self):
        p = self.p
        self.far.wait_recv()
        both = self.part[(1 - p.x) * 2 + p.c].astype(F32) + self.cbuf[0].astype(F32)
        self.held[...] = both.astype(BF)
        self.last = send(self.held, self.xbuf, self.sems, self.base + 2, p.across)

    def finish(self):
        self.near.wait_recv()
        own = self.part[self.p.t].astype(F32) + self.cbuf[1].astype(F32)
        self.last.wait_recv()
        total = own + self.xbuf[...].astype(F32)
        for copy in (self.far, self.near, self.last):
            copy.wait_send()
        return total


def block_of(ref, at):
    return ref.at[:, at] if len(ref.shape) == 4 else ref.at[at]


class WeightGather:
    def __init__(self, place, shard, full, zsem, ysem, lsem):
        p = self.p = place
        self.full, self.ysem = full, ysem
        own = block_of(full, p.d)
        self.zs = [send(shard, own, zsem, s - 1, p.z(s)) for s in range(1, p.outer)]
        self.ys = [send(shard, own, ysem, 0, p.y)]
        self.local = pltpu.make_async_copy(shard, own, lsem)
        self.local.start()

    def forward(self):
        p = self.p
        for s in range(1, p.outer):
            self.zs[s - 1].wait_recv()
            at = block_of(self.full, p.back(s) * 2 + p.i)
            self.ys.append(send(at, at, self.ysem, s, p.y))

    def finish(self):
        self.local.wait()
        for copy in self.ys:
            copy.wait_recv()

    def sent(self):
        for copy in self.zs + self.ys:
            copy.wait_send()


class GradScatter:
    def __init__(self, place, grads, ybuf, ysum, zbuf, zsem, ysem):
        p = self.p = place
        self.grads, self.ybuf, self.ysum, self.zbuf, self.zsem = grads, ybuf, ysum, zbuf, zsem
        self.ys = {}
        for s in self.order():
            block = block_of(grads, p.ahead(s) * 2 + 1 - p.i)
            self.ys[s] = send(block, ybuf.at[s], ysem, s, p.y)
        self.zs = []

    def order(self):
        return list(range(1, self.p.outer)) + [0]

    def pair(self, s):
        self.ys[s].wait_recv()
        own = block_of(self.grads, self.p.ahead(s) * 2 + self.p.i)
        return own[...].astype(F32) + self.ybuf[s].astype(F32)

    def forward(self):
        p = self.p
        for s in range(1, p.outer):
            self.ysum[s - 1] = self.pair(s).astype(BF)
            self.zs.append(send(self.ysum.at[s - 1], self.zbuf.at[s - 1], self.zsem, s - 1, p.z(s)))

    def finish(self):
        total = self.pair(0)
        for s in range(1, self.p.outer):
            self.zs[s - 1].wait_recv()
            total = total + self.zbuf[s - 1].astype(F32)
        for copy in self.zs + list(self.ys.values()):
            copy.wait_send()
        return total


def first_kernel(dp, tn, x, g1, g2, cot, cs, sn, segc, segr, wa, we, ws,
                 fa, fe, fs, n1, n2, cotg, q_out, k_out, v_out, att, mid,
                 part, cbuf, held, xbuf, tsem, az, ay, ez, ey, sz, sy, lsem):
    p = Place(dp, tn)
    p.barrier()
    ga = WeightGather(p, wa, fa, az, ay, lsem.at[0])
    rows = x[...].astype(F32)
    hat, unused = normalize(rows)
    n1[p.t] = (hat * g1[...]).astype(BF)
    cotg[p.t] = cot[...]
    gn = TensorGather(p, n1, tsem, 0)
    ge = WeightGather(p, we, fe, ez, ey, lsem.at[1])
    gs = WeightGather(p, ws, fs, sz, sy, lsem.at[2])
    gn.forward()
    ga.forward()
    gn.finish()
    ga.finish()
    group = n1.shape[0] * n1.shape[1]
    width = q_out.shape[1]
    depth = fa.shape[0] * fa.shape[1]
    tokens = n1[...].reshape(group, depth)
    merged = dot(tokens, fa[:, :, : 3 * width].reshape(depth, 3 * width))
    for ref, at in ((q_out, 0), (k_out, 1)):
        piece = merged[:, at * width : (at + 1) * width]
        ref[...] = (piece * cs[...] + swap_halves(piece) * sn[...]).astype(BF)
    v_out[...] = merged[:, 2 * width :].astype(BF)
    gc = TensorGather(p, cotg, tsem, 3)
    size = min(128, group)
    wide = min(size + WINDOW, group)
    for h in range(width // HEAD_DIM):
        cols = slice(h * HEAD_DIM, (h + 1) * HEAD_DIM)
        for b in range(group // size):
            lo = key_start(b, size, group, wide)
            qr, kr = slice(b * size, (b + 1) * size), slice(lo, lo + wide)
            probs = band_probs(q_out[qr, cols], k_out[kr, cols], segc[qr], segr[:, kr], b * size, lo)
            att[qr, cols] = dot(probs.astype(BF), v_out[kr, cols]).astype(BF)
    out_t = fa[:, :, 3 * width :].reshape(depth, width)
    part[...] = dot(att[...], out_t, ((1,), (1,))).astype(BF).reshape(part.shape)
    rs = TensorScatter(p, part, cbuf, held, xbuf, tsem, 6)
    gc.forward()
    rs.forward()
    ge.forward()
    middle = rows + rs.finish()
    mid[...] = middle
    hat_two, unused = normalize(middle)
    n2[p.t] = (hat_two * g2[...]).astype(BF)
    gm = TensorGather(p, n2, tsem, 9)
    gs.forward()
    gm.forward()
    gm.finish()
    gc.finish()
    ge.finish()
    gs.finish()
    for gather in (ga, ge, gs):
        gather.sent()


def second_kernel(dp, tn, pm, pd, mid, cot, x, g1, g2, cs, sn, segc, segr, fa, n1, q_in, k_in, v_in,
                  att, gre, grs,
                  out, din, oa, oe, os_, gains,
                  gra, branch, part, cbuf, held, xbuf, dqkv, dat,
                  ya, sa, za, ye, se, ze, ys, ss, zs, tbuf, ybuf, zbuf, tsem,
                  az, ay, ez, ey, sz, sy, gsem):
    p = Place(dp, tn)
    p.barrier()
    rd = TensorScatter(p, pd, cbuf.at[0], held.at[0], xbuf.at[0], tsem, 0)
    rm = TensorScatter(p, pm, cbuf.at[1], held.at[1], xbuf.at[1], tsem, 3)
    se_ = [GradScatter(p, grs, ys, ss, zs, sz, sy), GradScatter(p, gre, ye, se, ze, ez, ey)]
    rd.forward()
    rm.forward()
    middle = mid[...]
    hat_two, inv_two = normalize(middle)
    back, gain_two = norm_back(rd.finish(), hat_two, inv_two, g2[...])
    dmid = cot[...].astype(F32) + back
    branch[p.t] = dmid.astype(BF)
    gb = TensorGather(p, branch, tsem, 6)
    out[...] = (middle + rm.finish()).astype(BF)
    gb.forward()
    gb.finish()
    group = n1.shape[0] * n1.shape[1]
    width = q_in.shape[1]
    depth = fa.shape[0] * fa.shape[1]
    da = branch[...].reshape(group, depth)
    dat[...] = dot(da, fa[:, :, 3 * width :].reshape(depth, width)).astype(BF)
    gra[:, :, 3 * width :] = dot(da, att[...], ((0,), (0,))).astype(BF).reshape(
        gra.shape[0], gra.shape[1], width)
    dqkv[:, width:] = jnp.zeros((group, 2 * width), F32)
    size = min(128, group)
    wide = min(size + WINDOW, group)
    for h in range(width // HEAD_DIM):
        qc, kc, vc = (slice(n * width + h * HEAD_DIM, n * width + (h + 1) * HEAD_DIM) for n in range(3))
        for b in range(group // size):
            lo = key_start(b, size, group, wide)
            qr, kr = slice(b * size, (b + 1) * size), slice(lo, lo + wide)
            q, k, v, g = q_in[qr, qc], k_in[kr, qc], v_in[kr, qc], dat[qr, qc]
            probs = band_probs(q, k, segc[qr], segr[:, kr], b * size, lo)
            dqkv[kr, vc] += dot(probs.astype(BF), g, ((0,), (0,)))
            dprobs = dot(g, v, ((1,), (1,)))
            inner = jnp.sum(dprobs * probs, axis=-1, keepdims=True)
            draw = (probs * (dprobs - inner) * HEAD_DIM ** (-0.5)).astype(BF)
            dqkv[qr, qc] = dot(draw, k)
            dqkv[kr, kc] += dot(draw, q, ((0,), (0,)))
    turned = []
    for at in range(2):
        piece = dqkv[:, at * width : (at + 1) * width]
        turned.append((piece * cs[...] - swap_halves(piece) * sn[...]).astype(BF))
    turned.append(dqkv[:, 2 * width :].astype(BF))
    fused = jnp.concatenate(turned, axis=1)
    part[...] = dot(fused, fa[:, :, : 3 * width].reshape(depth, 3 * width), ((1,), (1,))).astype(BF).reshape(part.shape)
    rn = TensorScatter(p, part, cbuf.at[2], held.at[2], xbuf.at[2], tsem, 9)
    tokens = n1[...].reshape(group, depth)
    gra[:, :, : 3 * width] = dot(tokens, fused, ((0,), (0,))).astype(BF).reshape(
        gra.shape[0], gra.shape[1], 3 * width)
    sca = GradScatter(p, gra, ya, sa, za, az, ay)
    for scatter in se_:
        scatter.forward()
    rn.forward()
    hat, inv = normalize(x[...].astype(F32))
    back, gain_one = norm_back(rn.finish(), hat, inv, g1[...])
    din[...] = dmid + back
    lines = lax.broadcasted_iota(jnp.int32, tbuf.shape[1:], 0)
    tbuf[p.t] = jnp.where(lines == 0, gain_one, jnp.where(lines == 1, gain_two, 0.0))
    gt = TensorGather(p, tbuf, tsem, 12)
    gt.forward()
    sca.forward()
    gt.finish()
    ybuf[p.i] = sum(tbuf[n] for n in range(tn))
    cy = send(ybuf.at[p.i], ybuf.at[p.i], gsem, 0, p.y)
    cy.wait_recv()
    zbuf[p.o] = ybuf[0] + ybuf[1]
    cz = [send(zbuf.at[p.o], zbuf.at[p.o], gsem, s, p.z(s)) for s in range(1, p.outer)]
    os_[...] = se_[0].finish()
    oe[...] = se_[1].finish()
    oa[...] = sca.finish()
    for copy in cz:
        copy.wait_recv()
    gains[...] = sum(zbuf[n] for n in range(p.outer))
    for copy in [cy] + cz:
        copy.wait_send()


def call(kernel, outs, scratch, number, args):
    vmem = pl.BlockSpec(memory_space=pltpu.VMEM)
    return pl.pallas_call(
        kernel,
        out_shape=outs,
        in_specs=[vmem] * len(args),
        out_specs=[vmem] * len(outs),
        scratch_shapes=scratch,
        compiler_params=pltpu.CompilerParams(
            collective_id=number, has_side_effects=True, vmem_limit_bytes=56 << 20
        ),
    )(*args)


def local(dp, tn, layer_input, segments, positions, first_gain, merged_weight, output_weight,
          second_gain, expand_weight, shrink_weight, cotangent):
    rows, unused, width = merged_weight.shape
    units = expand_weight.shape[2]
    here, depth = layer_input.shape
    group = segments.shape[0]
    outer = dp // 2
    half = HEAD_DIM // 2
    sds = jax.ShapeDtypeStruct
    frequency = rope_base ** (-2.0 * jnp.arange(half, dtype=F32) / HEAD_DIM)
    angles = positions.astype(F32)[:, None] * frequency[None, :]
    cosine, sine = jnp.cos(angles), jnp.sin(angles)
    cs = jnp.tile(jnp.concatenate([cosine, cosine], axis=1), (1, width // HEAD_DIM))
    sn = jnp.tile(jnp.concatenate([-sine, sine], axis=1), (1, width // HEAD_DIM))
    segc, segr = segments[:, None], segments[None, :]
    g1, g2 = first_gain[None], second_gain[None]
    wa = jnp.concatenate([merged_weight.reshape(rows, 3 * width), output_weight.T], axis=1)
    we = expand_weight.transpose(1, 0, 2)
    ws = shrink_weight.T
    side = wa.shape[1]
    dma = pltpu.SemaphoreType.DMA
    zsem, ysem = dma((2, outer - 1)), dma((2, outer))
    slab = (tn, here, depth)
    fa, fe, fs, n1, n2, cotg, q, k, v, att, mid = call(
        partial(first_kernel, dp, tn),
        [sds((dp, rows, side), BF), sds((2, dp, rows, units), BF), sds((dp, rows, units), BF),
         sds(slab, BF), sds(slab, BF), sds(slab, BF)]
        + [sds((group, width), BF)] * 4 + [sds((here, depth), F32)],
        [pltpu.VMEM(slab, BF), pltpu.VMEM((2, here, depth), BF), pltpu.VMEM((here, depth), BF),
         pltpu.VMEM((here, depth), BF), dma((2, 12)), zsem, ysem, zsem, ysem, zsem, ysem, dma((3,))],
        0, (layer_input, g1, g2, cotangent, cs, sn, segc, segr, wa, we, ws))

    tokens = n2.reshape(group, depth)
    grad_mlp = cotg.reshape(group, depth)
    expand = fe.reshape(2, depth, units)
    shrink_t = fs.reshape(depth, units)
    gate, up = dot(tokens, expand[0]), dot(tokens, expand[1])
    activated, gelu_back = jax.vjp(partial(jax.nn.gelu, approximate=False), gate)
    hidden = (activated * up).astype(BF)
    pm = dot(hidden, shrink_t, ((1,), (1,))).astype(BF).reshape(slab)
    grad_hidden = dot(grad_mlp, shrink_t)
    d_in = gelu_back(grad_hidden * up)[0].astype(BF)
    d_gate = (grad_hidden * activated).astype(BF)
    pd = (dot(d_in, expand[0], ((1,), (1,))) + dot(d_gate, expand[1], ((1,), (1,)))).astype(BF).reshape(slab)
    grs = dot(grad_mlp, hidden, ((0,), (0,))).astype(BF).reshape(dp, rows, units)
    gre = jnp.stack([dot(tokens, d_in, ((0,), (0,))).astype(BF), dot(tokens, d_gate, ((0,), (0,))).astype(BF)])
    gre = gre.reshape(2, dp, rows, units)

    def bufs(shape):
        return [pltpu.VMEM((outer,) + shape, BF)] + [pltpu.VMEM((outer - 1,) + shape, BF)] * 2

    out, din, oa, oe, os_, gains = call(
        partial(second_kernel, dp, tn),
        [sds((here, depth), BF), sds((here, depth), F32), sds((rows, side), F32),
         sds((2, rows, units), F32), sds((rows, units), F32), sds((8, depth), F32)],
        [pltpu.VMEM((dp, rows, side), BF), pltpu.VMEM(slab, BF), pltpu.VMEM(slab, BF),
         pltpu.VMEM((3, 2, here, depth), BF), pltpu.VMEM((3, here, depth), BF),
         pltpu.VMEM((3, here, depth), BF), pltpu.VMEM((group, 3 * width), F32),
         pltpu.VMEM((group, width), BF)]
        + bufs((rows, side)) + bufs((2, rows, units)) + bufs((rows, units))
        + [pltpu.VMEM((tn, 8, depth), F32), pltpu.VMEM((2, 8, depth), F32),
           pltpu.VMEM((outer, 8, depth), F32), dma((2, 15)),
           zsem, ysem, zsem, ysem, zsem, ysem, ysem],
        1, (pm, pd, mid, cotangent, layer_input, g1, g2, cs, sn, segc, segr, fa, n1, q, k, v, att, gre, grs))
    return (out, din, gains[0], oa[:, : 3 * width].reshape(rows, 3, width), oa[:, 3 * width :].T,
            gains[1], oe.transpose(1, 0, 2), os_.T)


def solution(mesh):
    placed = (
        P(("dp", "tensor"), None), P("dp"), P("dp"), P(), P("dp", None, "tensor"), P("tensor", "dp"),
        P(), P("dp", None, "tensor"), P("tensor", "dp"), P(("dp", "tensor"), None),
    )
    return jax.shard_map(
        partial(local, mesh.shape["dp"], mesh.shape["tensor"]),
        mesh=mesh,
        in_specs=placed,
        out_specs=(
            P(("dp", "tensor"), None), P(("dp", "tensor"), None), P(), P("dp", None, "tensor"),
            P("tensor", "dp"), P(), P("dp", None, "tensor"), P("tensor", "dp"),
        ),
        check_vma=False,
    )
```
